128 devices in a mesh: dp: 16 (over y, x), tensor: 8 (over z, core).
Axes of the slice: x: 4, y: 4, z: 4, core: 2. Of those that a mesh axis runs over, the one named last changes fastest.
Arguments:
- activations: bfloat16 [16384, 8192], P('dp', 'tensor'), may hold values from -6 to 6
- out_grad: bfloat16 [16384, 5120], P('dp', 'tensor'), may hold values from -0.119628906 to 0.119628906
- counts: int32 [16], replicated, may hold values from 128 to 1024, as said below
Outputs:
- weight_grad: float32 [8192, 5120], P('dp', 'tensor')
- bias_grad: float32 [5120], P('tensor')
The draws below stay inside these ranges and needn't reach their ends.
Inputs may be any that keep to these rules, and one draw needn't show every extreme that they name: `counts`: every entry is a multiple of 128; some rank has all 1024 rows live in every draw.
All inputs are finite; a program needn't handle non-finite values.
Results may differ from the reference program's by a relative error of at most 0.0003.
Values may be sent and summed in bfloat16 or wider, within the bound.
No kernel may reach another device: no remote copies, remote signals or barrier semaphores. Data moves between devices by JAX's collectives and lax.ppermute only.
A program may use at most 128 MiB of HBM per device.

```python
import jax
import jax.numpy as jnp
from jax import lax

D = 8192
OUT = 5120
BLK = 128
CAP = 1024
TOKENS = 16384
RANKS = 16


def draw_counts(key, part):
    key = jax.random.fold_in(key, 11)
    first_key, second_key, third_key = jax.random.split(key, 3)
    blocks_total = CAP // BLK
    draw_one = jax.random.randint(first_key, (RANKS,), 1, blocks_total + 1)
    second = jax.random.randint(second_key, (RANKS,), 1, blocks_total + 1)
    heaviest = jax.random.randint(third_key, (), 0, RANKS)
    blocks = jnp.where(jnp.arange(RANKS) == heaviest, blocks_total, jnp.minimum(draw_one, second))
    return (blocks * BLK).astype(jnp.int32)


def block_levels(rng, shape, cuts, least, largest):
    gain = 1.0
    for dim, shards_of in cuts:
        steps = jax.random.uniform(jax.random.fold_in(jax.random.fold_in(rng, 6), dim), (shards_of,), jnp.float32, least / len(cuts), largest / len(cuts))
        gain = gain * jnp.repeat(jnp.exp(steps), shape[dim] // shards_of).reshape((-1,) + (1,) * (len(shape) - 1 - dim))
    return gain


def noise(key, dims, width, reach, cuts=(), kind=jnp.bfloat16):
    level = block_levels(key, dims, cuts, -0.22, 0.18) if cuts else 1.0
    result = jax.random.normal(key, dims, jnp.float32) * width * level
    return jnp.minimum(jnp.maximum(result, -reach), reach).astype(kind)


def setup_inputs(seed: int = 0) -> dict:
    streams_of = jax.random.split(jax.random.key(seed), 4)
    return {
        "activations": noise(streams_of[0], (TOKENS, D), 1.0, 6.0, ((0, 16), (1, 8))),
        "out_grad": noise(streams_of[1], (TOKENS, OUT), 0.02, 0.119628906, ((0, 16), (1, 8))),
        "counts": draw_counts(jax.random.fold_in(streams_of[3], 71), 0),
    }


def reference(activations, out_grad, counts):
    row_index = jnp.arange(TOKENS, dtype=jnp.int32)
    owner_rank = (row_index // CAP).astype(jnp.int32)
    position = row_index - owner_rank * CAP
    limits = jnp.take(counts, owner_rank)
    masked = jnp.where((position < limits)[:, None], out_grad, jnp.zeros_like(out_grad))
    weight_grad = jnp.dot(activations.astype(jnp.float32).T, masked.astype(jnp.float32), precision=lax.Precision.HIGHEST, preferred_element_type=jnp.float32)
    bias_grad = jnp.sum(masked.astype(jnp.float32), axis=0)
    return weight_grad, bias_grad
```

```python
import jax
import jax.numpy as jnp
from jax import lax
from jax.sharding import PartitionSpec as P


def per_device(activations, out_grad, counts):
    own_rank = lax.axis_index("dp")
    row_index = jnp.arange(out_grad.shape[0], dtype=jnp.int32)
    masked = jnp.where((row_index < counts[own_rank])[:, None], out_grad, jnp.zeros_like(out_grad))
    column_sums = jnp.sum(masked.astype(jnp.float32), axis=0)
    bias_grad = lax.psum(column_sums, "dp")
    features = lax.all_gather(activations, "tensor", axis=1, tiled=True)
    partial = lax.dot_general(
        features, masked, (((0,), (0,)), ((), ())), preferred_element_type=jnp.float32
    )
    weight_grad = lax.psum_scatter(partial, "dp", scatter_dimension=0, tiled=True)
    return (weight_grad, bias_grad)


def solution(mesh):
    in_specs = (P("dp", "tensor"), P("dp", "tensor"), P())
    out_specs = (P("dp", "tensor"), P("tensor"))
    return jax.shard_map(
        per_device, mesh=mesh, in_specs=in_specs, out_specs=out_specs, check_vma=False
    )
```

```python
import functools

import jax
import jax.numpy as jnp
from jax import lax
from jax.experimental import pallas as pl
from jax.experimental.pallas import tpu as pltpu
from jax.sharding import PartitionSpec as P

SIDE = 4
LANES = 128
TILE = 16
EXTRA = 2 * TILE
FINE = 2.0**-15
STEPS = 128.0
TOP = 32700.0
AXES = ("dp", "tensor")
PARAMS = pltpu.CompilerParams(vmem_limit_bytes=20 * 1024 * 1024)


def place(y, x, z, c):
    return ((y % SIDE * SIDE + x % SIDE) * SIDE + z % SIDE) * 2 + c % 2


def pairs(move):
    return [
        (place(y, x, z, c), place(*move(y, x, z, c)))
        for y in range(SIDE)
        for x in range(SIDE)
        for z in range(SIDE)
        for c in range(2)
    ]


def to_owner(step):
    def move(y, x, z, c):
        if c == (x + step) % SIDE // 2:
            return y, x + step, z, 0
        return y, x + step + 2, z, 1

    return pairs(move)


TO_OWNER = [to_owner(step) for step in range(2)]
RING_X = pairs(lambda y, x, z, c: (y, x + 1 - 2 * c, z, c))
RING_Z = pairs(lambda y, x, z, c: (y, x, z + 1 - 2 * c, c))
SWAP = pairs(lambda y, x, z, c: (y, x, z, c + 1))
ALONG_Y = [
    [place(y, x, z, c) for y in range(SIDE)] for x in range(SIDE) for z in range(SIDE) for c in range(2)
]


AWAY_Y = [pairs(lambda y, x, z, c, d=d: (y + d, x, z, c)) for d in range(SIDE)]


def send(value, perm):
    return lax.ppermute(value, AXES, perm)


def after(value, *others):
    return lax.optimization_barrier((value, *others))[0]


def scale_of(top):
    return jnp.ceil(jnp.log2(jnp.maximum(top, 2.0**-100) * (1.0 / TOP)) * STEPS)


def pack(total, bias, out, where):
    rows = total.shape[0]
    step = scale_of(jnp.max(jnp.abs(total), axis=0, keepdims=True))
    coded = jnp.round(total * jnp.exp2(step * (-1.0 / STEPS))).astype(jnp.int32)
    out[(*where, slice(0, rows))] = coded.astype(jnp.int16)
    row = lax.broadcasted_iota(jnp.int32, (TILE, LANES), 0)
    steps = jnp.broadcast_to(step, (TILE, LANES))
    if bias is None:
        out[(*where, slice(rows, rows + TILE))] = steps.astype(jnp.int32).astype(jnp.int16)
        return
    bias_step = jnp.broadcast_to(scale_of(jnp.max(jnp.abs(bias), axis=0, keepdims=True)), bias.shape)
    scaled = bias * jnp.exp2(bias_step * (-1.0 / STEPS))
    high = jnp.round(scaled)
    low = jnp.round((scaled - high) * (1.0 / FINE))
    head = jnp.where(row == 0, steps, high)
    tail = jnp.where(row == 0, bias_step, low)
    out[(*where, slice(rows, rows + TILE))] = head.astype(jnp.int32).astype(jnp.int16)
    out[(*where, slice(rows + TILE, rows + EXTRA))] = tail.astype(jnp.int32).astype(jnp.int16)


def wide(message, where, start, rows):
    return message[(*where, slice(start, start + rows))].astype(jnp.int32).astype(jnp.float32)


def unpack(message, where, rows):
    step = wide(message, where, rows, TILE)[0:1]
    return wide(message, where, 0, rows) * jnp.exp2(step * (1.0 / STEPS))


def unpack_bias(message, where, rows):
    high, low = wide(message, where, rows, TILE), wide(message, where, rows + TILE, TILE)
    row = lax.broadcasted_iota(jnp.int32, (TILE, LANES), 0)
    step = jnp.broadcast_to(low[0:1], (TILE, LANES))
    return jnp.where(row == 0, 0.0, (high + low * FINE) * jnp.exp2(step * (1.0 / STEPS)))


def cut(first, halves, activations, *outs):
    half_columns = activations.shape[1] // 2
    for step, out in enumerate(outs):
        start = pl.multiple_of(halves[step] * half_columns + first, LANES)
        out[...] = activations[:, pl.ds(start, out.shape[1])]


def join(near, far, out):
    tokens = near.shape[0]
    out[0:tokens, :] = near[...]
    out[tokens:, :] = far[...]


def mask(count, out_grad, grads):
    tokens, width = out_grad.shape
    row = lax.broadcasted_iota(jnp.int32, (tokens, LANES), 0)
    for number in range(width // LANES):
        span = slice(number * LANES, (number + 1) * LANES)
        masked = jnp.where(row < count[0], out_grad[:, span].astype(jnp.float32), 0.0)
        grads[span, :] = masked.T.astype(jnp.bfloat16)


def multiply(with_bias, table, *refs):
    grads, held, other = refs[:SIDE], refs[SIDE : 2 * SIDE], refs[2 * SIDE : 3 * SIDE]
    out = refs[-1]
    width, tokens = grads[0].shape
    sums_of_rows = None
    if with_bias:
        ones = jnp.ones((TILE, tokens), jnp.bfloat16)
        sums = sum(
            lax.dot_general(ones, g[...], (((1,), (1,)), ((), ())), preferred_element_type=jnp.float32)
            for g in grads
        )
        row = lax.broadcasted_iota(jnp.int32, (TILE, LANES), 0)
        sums_of_rows = jnp.zeros((TILE, LANES), jnp.float32)
        for number in range(width // LANES):
            span = slice(number * LANES, (number + 1) * LANES)
            sums_of_rows = jnp.where(row == number + 1, sums[:, span], sums_of_rows)
    for slot in range(SIDE):
        factors = [
            (ref, start)
            for ref in (held[slot], other[-slot % SIDE])
            for start in (0, tokens)
        ]
        total = sum(
            jnp.dot(g[...], ref[start : start + tokens, :], preferred_element_type=jnp.float32)
            for g, (ref, start) in zip(grads, factors, strict=True)
        )
        for part in range(total.shape[1] // LANES):
            bias = sums_of_rows if part == 0 else None
            pack(total[:, part * LANES : (part + 1) * LANES], bias, out, (table[slot], part))


def reduce(counts, *refs):
    messages, (out, bias_out) = refs[:-2], refs[-2:]
    rows = messages[0].shape[-2] - EXTRA
    at = 0
    for count in counts:
        mine, messages = messages[:count], messages[count:]
        sources = [(m, ()) for m in mine] if count > 1 else [(mine[0], (n,)) for n in range(SIDE)]
        if at == 0:
            bias_out[...] = sum(unpack_bias(m, (*n, 0), rows) for m, n in sources)
        for part in range(mine[0].shape[-3]):
            total = sum(unpack(m, (*n, part), rows) for m, n in sources)
            out[at : at + LANES, :] = total.T
            at += LANES


def whole():
    return pl.BlockSpec(memory_space=pltpu.VMEM)


def scalars():
    return pl.BlockSpec(memory_space=pltpu.SMEM)


def shape(dtype, *dims):
    return jax.ShapeDtypeStruct(dims, dtype)


def kernel(body, out_shape, scalar, *values, scratch=()):
    return pl.pallas_call(
        body,
        out_shape=out_shape,
        in_specs=[scalars()] * (scalar is not None) + [whole()] * len(values),
        out_specs=[whole()] * len(out_shape),
        scratch_shapes=scratch,
        compiler_params=PARAMS,
    )(*([] if scalar is None else [scalar]), *values)


def per_device(activations, out_grad, counts):
    rank, column = lax.axis_index("dp"), lax.axis_index("tensor")
    y, x, z, c = rank // SIDE, rank % SIDE, column // 2, column % 2
    tokens, width = out_grad.shape
    columns = activations.shape[1] // 4
    parts = columns // LANES
    slots = jnp.arange(SIDE)
    owners = (jnp.where(c == 0, z - slots, z + slots) % SIDE).astype(jnp.int32)
    owners_away = ((owners - y) % SIDE).astype(jnp.int32)
    halves = jnp.stack([x % 2, 1 - x % 2]).astype(jnp.int32)

    def cut_columns(first, value):
        out = [shape(value.dtype, tokens, columns)] * 2
        return kernel(functools.partial(cut, first), out, halves, value)

    def to_owners(cuts):
        got = [send(piece, perm) for piece, perm in zip(cuts, TO_OWNER, strict=True)]
        return kernel(join, [shape(got[0].dtype, 2 * tokens, columns)], None, *got)[0]

    def sums(table, grads, held, other, with_bias):
        (message,) = kernel(
            functools.partial(multiply, with_bias),
            [shape(jnp.int16, SIDE, parts, width + EXTRA, LANES)],
            table,
            *grads,
            *held,
            *other,
        )
        return message

    cuts = cut_columns(0, activations)
    (grad,) = kernel(
        mask,
        [shape(jnp.bfloat16, width, tokens)],
        counts[rank].reshape(1),
        after(out_grad, *cuts),
    )
    more = cut_columns(columns, after(activations, *cuts))
    own = [to_owners(cuts)]
    own.append(to_owners([after(piece, own[0]) for piece in more]))
    ring = [[piece, send(piece, RING_Z)] for piece in own]
    other = [[send(piece, SWAP)] for piece in own]
    grads = [grad]
    for step in range(SIDE - 1):
        grads.append(send(after(grads[-1], *own), RING_X))
    for step in (1, 2):
        for run in range(2):
            piece = ring[run][step]
            ring[run].append(send(after(piece, other[run][step - 1]), RING_Z))
            other[run].append(send(piece, SWAP))
    for run in range(2):
        other[run].append(send(ring[run][3], SWAP))
    first = c == 0
    near, far = jnp.where(first, grads[0], grads[2]), jnp.where(first, grads[2], grads[0])
    grads = [near, grads[1], far, grads[3]]
    early = sums(owners_away, grads, ring[0], other[0], True)
    late = sums(owners, grads, [after(ring[1][0], early), *ring[1][1:]], other[1], False)
    messages = [
        [early[0]] + [send(early[d], AWAY_Y[d]) for d in range(1, SIDE)],
        [lax.all_to_all(late, AXES, 0, 0, axis_index_groups=ALONG_Y, tiled=True)],
    ]
    weight_grad, bias = kernel(
        functools.partial(reduce, tuple(map(len, messages))),
        [shape(jnp.float32, 2 * columns, width), shape(jnp.float32, TILE, LANES)],
        None,
        *messages[0],
        *messages[1],
    )
    return weight_grad, bias[1 : 1 + width // LANES].reshape(width)


def solution(mesh):
    in_specs = (P("dp", "tensor"), P("dp", "tensor"), P())
    out_specs = (P("dp", "tensor"), P("tensor"))
    return jax.shard_map(
        per_device, mesh=mesh, in_specs=in_specs, out_specs=out_specs, check_vma=False
    )
```

```python
import functools

import jax
import jax.numpy as jnp
from jax import lax
from jax.experimental import pallas as pl
from jax.experimental.pallas import tpu as pltpu
from jax.sharding import PartitionSpec as P

SIDE = 4
LANES = 128
TILE = 16
EXTRA = 2 * TILE
FINE = 2.0**-15
STEPS = 128.0
TOP = 32700.0
AXES = ("dp", "tensor")
PARAMS = pltpu.CompilerParams(vmem_limit_bytes=20 * 1024 * 1024)


def place(y, x, z, c):
    return ((y % SIDE * SIDE + x % SIDE) * SIDE + z % SIDE) * 2 + c % 2


def pairs(move):
    return [
        (place(y, x, z, c), place(*move(y, x, z, c)))
        for y in range(SIDE)
        for x in range(SIDE)
        for z in range(SIDE)
        for c in range(2)
    ]


def to_owner(step):
    def move(y, x, z, c):
        if c == (x + step) % SIDE // 2:
            return y, x + step, z, 0
        return y, x + step + 2, z, 1

    return pairs(move)


TO_OWNER = [to_owner(step) for step in range(2)]
RING_X = pairs(lambda y, x, z, c: (y, x + 1 - 2 * c, z, c))
RING_Z = pairs(lambda y, x, z, c: (y, x, z + 1 - 2 * c, c))
SWAP = pairs(lambda y, x, z, c: (y, x, z, c + 1))
ALONG_X = [
    [place(y, x, z, c) for x in range(SIDE)] for y in range(SIDE) for z in range(SIDE) for c in range(2)
]
ALONG_Y = [
    [place(y, x, z, c) for y in range(SIDE)] for x in range(SIDE) for z in range(SIDE) for c in range(2)
]


AWAY_Y = [pairs(lambda y, x, z, c, d=d: (y + d, x, z, c)) for d in range(SIDE)]


def send(value, perm):
    return lax.ppermute(value, AXES, perm)


def swap_all(value, groups):
    return lax.all_to_all(value, AXES, 0, 0, axis_index_groups=groups, tiled=True)


def after(value, *others):
    return lax.optimization_barrier((value, *others))[0]


def scale_of(top):
    return jnp.ceil(jnp.log2(jnp.maximum(top, 2.0**-100) * (1.0 / TOP)) * STEPS)


def pack(total, bias, out, where):
    rows = total.shape[0]
    step = scale_of(jnp.max(jnp.abs(total), axis=0, keepdims=True))
    coded = jnp.round(total * jnp.exp2(step * (-1.0 / STEPS))).astype(jnp.int32)
    out[(*where, slice(0, rows))] = coded.astype(jnp.int16)
    row = lax.broadcasted_iota(jnp.int32, (TILE, LANES), 0)
    steps = jnp.broadcast_to(step, (TILE, LANES))
    if bias is None:
        out[(*where, slice(rows, rows + TILE))] = steps.astype(jnp.int32).astype(jnp.int16)
        return
    bias_step = jnp.broadcast_to(scale_of(jnp.max(jnp.abs(bias), axis=0, keepdims=True)), bias.shape)
    scaled = bias * jnp.exp2(bias_step * (-1.0 / STEPS))
    high = jnp.round(scaled)
    low = jnp.round((scaled - high) * (1.0 / FINE))
    head = jnp.where(row == 0, steps, high)
    tail = jnp.where(row == 0, bias_step, low)
    out[(*where, slice(rows, rows + TILE))] = head.astype(jnp.int32).astype(jnp.int16)
    out[(*where, slice(rows + TILE, rows + EXTRA))] = tail.astype(jnp.int32).astype(jnp.int16)


def wide(message, where, start, rows):
    return message[(*where, slice(start, start + rows))].astype(jnp.int32).astype(jnp.float32)


def unpack(message, where, rows):
    step = wide(message, where, rows, TILE)[0:1]
    return wide(message, where, 0, rows) * jnp.exp2(step * (1.0 / STEPS))


def unpack_bias(message, where, rows):
    high, low = wide(message, where, rows, TILE), wide(message, where, rows + TILE, TILE)
    row = lax.broadcasted_iota(jnp.int32, (TILE, LANES), 0)
    step = jnp.broadcast_to(low[0:1], (TILE, LANES))
    return jnp.where(row == 0, 0.0, (high + low * FINE) * jnp.exp2(step * (1.0 / STEPS)))


def cut(halves, activations, *outs):
    half_columns = activations.shape[1] // 2
    for number, out in enumerate(outs):
        run, step = number // 2, number % 2
        start = pl.multiple_of(halves[step] * half_columns + run * out.shape[1], LANES)
        out[...] = activations[:, pl.ds(start, out.shape[1])]


def join(near, far, out):
    tokens = near.shape[0]
    out[0:tokens, :] = near[...]
    out[tokens:, :] = far[...]


def mask(count, out_grad, grads):
    tokens, width = out_grad.shape
    row = lax.broadcasted_iota(jnp.int32, (tokens, LANES), 0)
    for number in range(width // LANES):
        span = slice(number * LANES, (number + 1) * LANES)
        masked = jnp.where(row < count[0], out_grad[:, span].astype(jnp.float32), 0.0)
        turned = masked.T.astype(jnp.bfloat16)
        for copy in range(SIDE):
            grads[copy, span, :] = turned


def multiply(with_bias, table, grads, *refs):
    held, other, out = refs[:SIDE], refs[SIDE : 2 * SIDE], refs[-1]
    _, width, tokens = grads.shape
    sums_of_rows = None
    if with_bias:
        ones = jnp.ones((TILE, tokens), jnp.bfloat16)
        sums = sum(
            lax.dot_general(ones, grads[n], (((1,), (1,)), ((), ())), preferred_element_type=jnp.float32)
            for n in range(SIDE)
        )
        row = lax.broadcasted_iota(jnp.int32, (TILE, LANES), 0)
        sums_of_rows = jnp.zeros((TILE, LANES), jnp.float32)
        for number in range(width // LANES):
            span = slice(number * LANES, (number + 1) * LANES)
            sums_of_rows = jnp.where(row == number + 1, sums[:, span], sums_of_rows)
    for slot in range(SIDE):
        factors = [(ref, start) for ref in (held[slot], other[-slot % SIDE]) for start in (0, tokens)]
        total = sum(
            jnp.dot(
                grads[table[SIDE + n]], ref[start : start + tokens, :], preferred_element_type=jnp.float32
            )
            for n, (ref, start) in enumerate(factors)
        )
        for part in range(total.shape[1] // LANES):
            bias = sums_of_rows if part == 0 else None
            pack(total[:, part * LANES : (part + 1) * LANES], bias, out, (table[slot], part))


def reduce(counts, *refs):
    messages, (out, bias_out) = refs[:-2], refs[-2:]
    rows = messages[0].shape[-2] - EXTRA
    at = 0
    for count in counts:
        mine, messages = messages[:count], messages[count:]
        sources = [(m, ()) for m in mine] if count > 1 else [(mine[0], (n,)) for n in range(SIDE)]
        if at == 0:
            bias_out[...] = sum(unpack_bias(m, (*n, 0), rows) for m, n in sources)
        for part in range(mine[0].shape[-3]):
            total = sum(unpack(m, (*n, part), rows) for m, n in sources)
            out[at : at + LANES, :] = total.T
            at += LANES


def whole():
    return pl.BlockSpec(memory_space=pltpu.VMEM)


def scalars():
    return pl.BlockSpec(memory_space=pltpu.SMEM)


def shape(dtype, *dims):
    return jax.ShapeDtypeStruct(dims, dtype)


def kernel(body, out_shape, scalar, *values, scratch=()):
    return pl.pallas_call(
        body,
        out_shape=out_shape,
        in_specs=[scalars()] * (scalar is not None) + [whole()] * len(values),
        out_specs=[whole()] * len(out_shape),
        scratch_shapes=scratch,
        compiler_params=PARAMS,
    )(*([] if scalar is None else [scalar]), *values)


def per_device(activations, out_grad, counts):
    rank, column = lax.axis_index("dp"), lax.axis_index("tensor")
    y, x, z, c = rank // SIDE, rank % SIDE, column // 2, column % 2
    tokens, width = out_grad.shape
    columns = activations.shape[1] // 4
    parts = columns // LANES
    slots = jnp.arange(SIDE)
    owners = jnp.where(c == 0, z - slots, z + slots) % SIDE
    ranks = (x - slots - 2 * c) % SIDE
    tables = [
        jnp.concatenate([numbers, ranks]).astype(jnp.int32) for numbers in (owners, (owners - y) % SIDE)
    ]
    halves = jnp.stack([x % 2, 1 - x % 2]).astype(jnp.int32)

    def to_owners(cuts, *others):
        got = [send(piece, perm) for piece, perm in zip(cuts, TO_OWNER, strict=True)]
        got[0] = after(got[0], *others)
        return kernel(join, [shape(got[0].dtype, 2 * tokens, columns)], None, *got)[0]

    def sums(table, grads, held, other, with_bias):
        (message,) = kernel(
            functools.partial(multiply, with_bias),
            [shape(jnp.int16, SIDE, parts, width + EXTRA, LANES)],
            table,
            grads,
            *held,
            *other,
        )
        return message

    cuts = kernel(cut, [shape(activations.dtype, tokens, columns)] * 4, halves, activations)
    (grad,) = kernel(
        mask,
        [shape(jnp.bfloat16, SIDE, width, tokens)],
        counts[rank].reshape(1),
        after(out_grad, *cuts),
    )
    own = [to_owners(cuts[:2], grad), to_owners(cuts[2:])]
    ring = [[piece, send(piece, RING_Z)] for piece in own]
    grads = swap_all(after(grad, *own), ALONG_X)
    other = [[send(piece, SWAP)] for piece in own]
    ring[0].append(send(ring[0][1], RING_Z))
    other[0].append(send(ring[0][1], SWAP))
    ring[1].append(send(after(ring[1][1], other[0][0]), RING_Z))
    other[1].append(send(ring[1][1], SWAP))
    ring[0].append(send(after(ring[0][2], other[0][1]), RING_Z))
    other[0].append(send(ring[0][2], SWAP))
    ring[1].append(send(after(ring[1][2], *other[1], other[0][2]), RING_Z))
    other[1].append(send(ring[1][2], SWAP))
    other[0].append(send(ring[0][3], SWAP))
    early = sums(tables[0], grads, [after(ring[0][0], ring[1][2]), *ring[0][1:]], other[0], True)
    other[1].append(send(after(ring[1][3], early), SWAP))
    late = sums(tables[1], grads, ring[1], other[1], False)
    messages = [
        [swap_all(after(early, ring[1][3]), ALONG_Y)],
        [late[0]] + [send(late[d], AWAY_Y[d]) for d in range(1, SIDE)],
    ]
    weight_grad, bias = kernel(
        functools.partial(reduce, tuple(map(len, messages))),
        [shape(jnp.float32, 2 * columns, width), shape(jnp.float32, TILE, LANES)],
        None,
        *messages[0],
        *messages[1],
    )
    return weight_grad, bias[1 : 1 + width // LANES].reshape(width)


def solution(mesh):
    in_specs = (P("dp", "tensor"), P("dp", "tensor"), P())
    out_specs = (P("dp", "tensor"), P("tensor"))
    return jax.shard_map(
        per_device, mesh=mesh, in_specs=in_specs, out_specs=out_specs, check_vma=False
    )
```

```python
import functools

import jax
import jax.numpy as jnp
from jax import lax
from jax.experimental import pallas as pl
from jax.experimental.pallas import tpu as pltpu
from jax.sharding import PartitionSpec as P

SIDE = 4
LANES = 128
TILE = 16
EXTRA = 2 * TILE
FINE = 2.0**-15
STEPS = 128.0
TOP = 32700.0
AXES = ("dp", "tensor")
PARAMS = pltpu.CompilerParams(vmem_limit_bytes=20 * 1024 * 1024)


def place(y, x, z, c):
    return ((y % SIDE * SIDE + x % SIDE) * SIDE + z % SIDE) * 2 + c % 2


def pairs(move):
    return [
        (place(y, x, z, c), place(*move(y, x, z, c)))
        for y in range(SIDE)
        for x in range(SIDE)
        for z in range(SIDE)
        for c in range(2)
    ]


def to_owner(step):
    def move(y, x, z, c):
        if c == (x + step) % SIDE // 2:
            return y, x + step, z, 0
        return y, x + step + 2, z, 1

    return pairs(move)


TO_OWNER = [to_owner(step) for step in range(2)]
RING_X = pairs(lambda y, x, z, c: (y, x + 1 - 2 * c, z, c))
RING_Z = pairs(lambda y, x, z, c: (y, x, z + 1 - 2 * c, c))
SWAP = pairs(lambda y, x, z, c: (y, x, z, c + 1))
ALONG_X = [
    [place(y, x, z, c) for x in range(SIDE)] for y in range(SIDE) for z in range(SIDE) for c in range(2)
]
ALONG_Y = [
    [place(y, x, z, c) for y in range(SIDE)] for x in range(SIDE) for z in range(SIDE) for c in range(2)
]


AWAY_Y = [pairs(lambda y, x, z, c, d=d: (y + d, x, z, c)) for d in range(SIDE)]


def send(value, perm):
    return lax.ppermute(value, AXES, perm)


def swap_all(value, groups):
    return lax.all_to_all(value, AXES, 0, 0, axis_index_groups=groups, tiled=True)


def after(value, *others):
    return lax.optimization_barrier((value, *others))[0]


def scale_of(top):
    return jnp.ceil(jnp.log2(jnp.maximum(top, 2.0**-100) * (1.0 / TOP)) * STEPS)


def pack(total, bias, out, where):
    rows = total.shape[0]
    step = scale_of(jnp.max(jnp.abs(total), axis=0, keepdims=True))
    coded = jnp.round(total * jnp.exp2(step * (-1.0 / STEPS))).astype(jnp.int32)
    out[(*where, slice(0, rows))] = coded.astype(jnp.int16)
    row = lax.broadcasted_iota(jnp.int32, (TILE, LANES), 0)
    steps = jnp.broadcast_to(step, (TILE, LANES))
    if bias is None:
        out[(*where, slice(rows, rows + TILE))] = steps.astype(jnp.int32).astype(jnp.int16)
        return
    bias_step = jnp.broadcast_to(scale_of(jnp.max(jnp.abs(bias), axis=0, keepdims=True)), bias.shape)
    scaled = bias * jnp.exp2(bias_step * (-1.0 / STEPS))
    high = jnp.round(scaled)
    low = jnp.round((scaled - high) * (1.0 / FINE))
    head = jnp.where(row == 0, steps, high)
    tail = jnp.where(row == 0, bias_step, low)
    out[(*where, slice(rows, rows + TILE))] = head.astype(jnp.int32).astype(jnp.int16)
    out[(*where, slice(rows + TILE, rows + EXTRA))] = tail.astype(jnp.int32).astype(jnp.int16)


def wide(message, where, start, rows):
    return message[(*where, slice(start, start + rows))].astype(jnp.int32).astype(jnp.float32)


def unpack(message, where, rows):
    step = wide(message, where, rows, TILE)[0:1]
    return wide(message, where, 0, rows) * jnp.exp2(step * (1.0 / STEPS))


def unpack_bias(message, where, rows):
    high, low = wide(message, where, rows, TILE), wide(message, where, rows + TILE, TILE)
    row = lax.broadcasted_iota(jnp.int32, (TILE, LANES), 0)
    step = jnp.broadcast_to(low[0:1], (TILE, LANES))
    return jnp.where(row == 0, 0.0, (high + low * FINE) * jnp.exp2(step * (1.0 / STEPS)))


def cut(halves, activations, *outs):
    half_columns = activations.shape[1] // 2
    for number, out in enumerate(outs):
        run, step = number // 2, number % 2
        start = pl.multiple_of(halves[step] * half_columns + run * out.shape[1], LANES)
        out[...] = activations[:, pl.ds(start, out.shape[1])]


def join(near, far, out):
    tokens = near.shape[0]
    out[0:tokens, :] = near[...]
    out[tokens:, :] = far[...]


def mask(count, out_grad, grads):
    tokens, width = out_grad.shape
    row = lax.broadcasted_iota(jnp.int32, (tokens, LANES), 0)
    for number in range(width // LANES):
        span = slice(number * LANES, (number + 1) * LANES)
        masked = jnp.where(row < count[0], out_grad[:, span].astype(jnp.float32), 0.0)
        turned = masked.T.astype(jnp.bfloat16)
        for copy in range(SIDE):
            grads[copy, span, :] = turned


def multiply(with_bias, table, grads, *refs):
    held, other, out = refs[:SIDE], refs[SIDE : 2 * SIDE], refs[-1]
    _, width, tokens = grads.shape
    sums_of_rows = None
    if with_bias:
        ones = jnp.ones((TILE, tokens), jnp.bfloat16)
        sums = sum(
            lax.dot_general(ones, grads[n], (((1,), (1,)), ((), ())), preferred_element_type=jnp.float32)
            for n in range(SIDE)
        )
        row = lax.broadcasted_iota(jnp.int32, (TILE, LANES), 0)
        sums_of_rows = jnp.zeros((TILE, LANES), jnp.float32)
        for number in range(width // LANES):
            span = slice(number * LANES, (number + 1) * LANES)
            sums_of_rows = jnp.where(row == number + 1, sums[:, span], sums_of_rows)
    for slot in range(SIDE):
        factors = [(ref, start) for ref in (held[slot], other[-slot % SIDE]) for start in (0, tokens)]
        total = sum(
            jnp.dot(
                grads[table[SIDE + n]], ref[start : start + tokens, :], preferred_element_type=jnp.float32
            )
            for n, (ref, start) in enumerate(factors)
        )
        for part in range(total.shape[1] // LANES):
            bias = sums_of_rows if part == 0 else None
            pack(total[:, part * LANES : (part + 1) * LANES], bias, out, (table[slot], part))


def reduce(counts, *refs):
    messages, (out, bias_out) = refs[:-2], refs[-2:]
    rows = out.shape[1]
    at = 0
    for count in counts:
        mine, messages = messages[:count], messages[count:]
        sources = [(m, ()) for m in mine] if count > 1 else [(mine[0], (n,)) for n in range(SIDE)]
        if mine[0].shape[-2] == rows + EXTRA:
            bias_out[...] = sum(unpack_bias(m, (*n, 0), rows) for m, n in sources)
        for part in range(mine[0].shape[-3]):
            total = sum(unpack(m, (*n, part), rows) for m, n in sources)
            out[at : at + LANES, :] = total.T
            at += LANES


def whole():
    return pl.BlockSpec(memory_space=pltpu.VMEM)


def scalars():
    return pl.BlockSpec(memory_space=pltpu.SMEM)


def shape(dtype, *dims):
    return jax.ShapeDtypeStruct(dims, dtype)


def kernel(body, out_shape, scalar, *values, scratch=()):
    return pl.pallas_call(
        body,
        out_shape=out_shape,
        in_specs=[scalars()] * (scalar is not None) + [whole()] * len(values),
        out_specs=[whole()] * len(out_shape),
        scratch_shapes=scratch,
        compiler_params=PARAMS,
    )(*([] if scalar is None else [scalar]), *values)


def per_device(activations, out_grad, counts):
    rank, column = lax.axis_index("dp"), lax.axis_index("tensor")
    y, x, z, c = rank // SIDE, rank % SIDE, column // 2, column % 2
    tokens, width = out_grad.shape
    columns = activations.shape[1] // 4
    parts = columns // LANES
    slots = jnp.arange(SIDE)
    owners = jnp.where(c == 0, z - slots, z + slots) % SIDE
    ranks = (x - slots - 2 * c) % SIDE
    tables = [
        jnp.concatenate([numbers, ranks]).astype(jnp.int32) for numbers in (owners, (owners - y) % SIDE)
    ]
    halves = jnp.stack([x % 2, 1 - x % 2]).astype(jnp.int32)

    def to_owners(cuts, *others):
        got = [send(piece, perm) for piece, perm in zip(cuts, TO_OWNER, strict=True)]
        got[0] = after(got[0], *others)
        return kernel(join, [shape(got[0].dtype, 2 * tokens, columns)], None, *got)[0]

    def sums(table, grads, held, other, with_bias):
        (message,) = kernel(
            functools.partial(multiply, with_bias),
            [shape(jnp.int16, SIDE, parts, width + (EXTRA if with_bias else TILE), LANES)],
            table,
            grads,
            *held,
            *other,
        )
        return message

    cuts = kernel(cut, [shape(activations.dtype, tokens, columns)] * 4, halves, activations)
    (grad,) = kernel(
        mask,
        [shape(jnp.bfloat16, SIDE, width, tokens)],
        counts[rank].reshape(1),
        after(out_grad, *cuts),
    )
    own = [to_owners(cuts[:2], grad), to_owners(cuts[2:])]
    ring = [[piece, send(piece, RING_Z)] for piece in own]
    grads = swap_all(after(grad, *own), ALONG_X)
    other = [[send(piece, SWAP)] for piece in own]
    ring[0].append(send(ring[0][1], RING_Z))
    other[0].append(send(ring[0][1], SWAP))
    ring[1].append(send(after(ring[1][1], other[0][0]), RING_Z))
    other[1].append(send(ring[1][1], SWAP))
    ring[0].append(send(after(ring[0][2], other[0][1]), RING_Z))
    other[0].append(send(ring[0][2], SWAP))
    ring[1].append(send(after(ring[1][2], *other[1], other[0][2]), RING_Z))
    other[1].append(send(ring[1][2], SWAP))
    other[0].append(send(ring[0][3], SWAP))
    early = sums(tables[0], grads, [after(ring[0][0], ring[1][2]), *ring[0][1:]], other[0], False)
    other[1].append(send(after(ring[1][3], early), SWAP))
    late = sums(tables[1], grads, ring[1], other[1], True)
    messages = [
        [swap_all(after(early, ring[1][3]), ALONG_Y)],
        [late[0]] + [send(late[d], AWAY_Y[d]) for d in range(1, SIDE)],
    ]
    weight_grad, bias = kernel(
        functools.partial(reduce, tuple(map(len, messages))),
        [shape(jnp.float32, 2 * columns, width), shape(jnp.float32, TILE, LANES)],
        None,
        *messages[0],
        *messages[1],
    )
    return weight_grad, bias[1 : 1 + width // LANES].reshape(width)


def solution(mesh):
    in_specs = (P("dp", "tensor"), P("dp", "tensor"), P())
    out_specs = (P("dp", "tensor"), P("tensor"))
    return jax.shard_map(
        per_device, mesh=mesh, in_specs=in_specs, out_specs=out_specs, check_vma=False
    )
```

```python
import functools

import jax
import jax.numpy as jnp
from jax import lax
from jax.experimental import pallas as pl
from jax.experimental.pallas import tpu as pltpu
from jax.sharding import PartitionSpec as P

SIDE = 4
LANES = 128
TILE = 16
EXTRA = 2 * TILE
FINE = 2.0**-15
STEPS = 128.0
TOP = 32700.0
AXES = ("dp", "tensor")
PARAMS = pltpu.CompilerParams(vmem_limit_bytes=20 * 1024 * 1024)


def place(y, x, z, c):
    return ((y % SIDE * SIDE + x % SIDE) * SIDE + z % SIDE) * 2 + c % 2


def pairs(move):
    return [
        (place(y, x, z, c), place(*move(y, x, z, c)))
        for y in range(SIDE)
        for x in range(SIDE)
        for z in range(SIDE)
        for c in range(2)
    ]


def to_owner(step):
    def move(y, x, z, c):
        if c == (x + step) % SIDE // 2:
            return y, x + step, z, 0
        return y, x + step + 2, z, 1

    return pairs(move)


TO_OWNER = [to_owner(step) for step in range(2)]
RING_X = pairs(lambda y, x, z, c: (y, x + 1 - 2 * c, z, c))
RING_Z = pairs(lambda y, x, z, c: (y, x, z + 1 - 2 * c, c))
SWAP = pairs(lambda y, x, z, c: (y, x, z, c + 1))
ALONG_X = [
    [place(y, x, z, c) for x in range(SIDE)] for y in range(SIDE) for z in range(SIDE) for c in range(2)
]
ALONG_Y = [
    [place(y, x, z, c) for y in range(SIDE)] for x in range(SIDE) for z in range(SIDE) for c in range(2)
]


AWAY_Y = [pairs(lambda y, x, z, c, d=d: (y + d, x, z, c)) for d in range(SIDE)]


def send(value, perm):
    return lax.ppermute(value, AXES, perm)


def swap_all(value, groups):
    return lax.all_to_all(value, AXES, 0, 0, axis_index_groups=groups, tiled=True)


def after(value, *others):
    return lax.optimization_barrier((value, *others))[0]


def scale_of(top):
    return jnp.ceil(jnp.log2(jnp.maximum(top, 2.0**-100) * (1.0 / TOP)) * STEPS)


def pack(total, bias, out, where):
    rows = total.shape[0]
    step = scale_of(jnp.max(jnp.abs(total), axis=0, keepdims=True))
    coded = jnp.round(total * jnp.exp2(step * (-1.0 / STEPS))).astype(jnp.int32)
    out[(*where, slice(0, rows))] = coded.astype(jnp.int16)
    row = lax.broadcasted_iota(jnp.int32, (TILE, LANES), 0)
    steps = jnp.broadcast_to(step, (TILE, LANES))
    if bias is None:
        out[(*where, slice(rows, rows + TILE))] = steps.astype(jnp.int32).astype(jnp.int16)
        return
    bias_step = jnp.broadcast_to(scale_of(jnp.max(jnp.abs(bias), axis=0, keepdims=True)), bias.shape)
    scaled = bias * jnp.exp2(bias_step * (-1.0 / STEPS))
    high = jnp.round(scaled)
    low = jnp.round((scaled - high) * (1.0 / FINE))
    head = jnp.where(row == 0, steps, high)
    tail = jnp.where(row == 0, bias_step, low)
    out[(*where, slice(rows, rows + TILE))] = head.astype(jnp.int32).astype(jnp.int16)
    out[(*where, slice(rows + TILE, rows + EXTRA))] = tail.astype(jnp.int32).astype(jnp.int16)


def wide(message, where, start, rows):
    return message[(*where, slice(start, start + rows))].astype(jnp.int32).astype(jnp.float32)


def unpack(message, where, rows):
    step = wide(message, where, rows, TILE)[0:1]
    return wide(message, where, 0, rows) * jnp.exp2(step * (1.0 / STEPS))


def unpack_bias(message, where, rows):
    high, low = wide(message, where, rows, TILE), wide(message, where, rows + TILE, TILE)
    row = lax.broadcasted_iota(jnp.int32, (TILE, LANES), 0)
    step = jnp.broadcast_to(low[0:1], (TILE, LANES))
    return jnp.where(row == 0, 0.0, (high + low * FINE) * jnp.exp2(step * (1.0 / STEPS)))


def cut(halves, activations, *outs):
    half_columns = activations.shape[1] // 2
    for number, out in enumerate(outs):
        run, step = number // 2, number % 2
        start = pl.multiple_of(halves[step] * half_columns + run * out.shape[1], LANES)
        out[...] = activations[:, pl.ds(start, out.shape[1])]


def join(near, far, out):
    tokens = near.shape[0]
    out[0:tokens, :] = near[...]
    out[tokens:, :] = far[...]


def mask(count, out_grad, grads):
    tokens, width = out_grad.shape
    row = lax.broadcasted_iota(jnp.int32, (tokens, LANES), 0)
    for number in range(width // LANES):
        span = slice(number * LANES, (number + 1) * LANES)
        masked = jnp.where(row < count[0], out_grad[:, span].astype(jnp.float32), 0.0)
        turned = masked.T.astype(jnp.bfloat16)
        for copy in range(SIDE):
            grads[copy, span, :] = turned


def multiply(with_bias, table, grads, *refs):
    held, other, out = refs[:SIDE], refs[SIDE : 2 * SIDE], refs[-1]
    _, width, tokens = grads.shape
    sums_of_rows = None
    if with_bias:
        ones = jnp.ones((TILE, tokens), jnp.bfloat16)
        sums = sum(
            lax.dot_general(ones, grads[n], (((1,), (1,)), ((), ())), preferred_element_type=jnp.float32)
            for n in range(SIDE)
        )
        row = lax.broadcasted_iota(jnp.int32, (TILE, LANES), 0)
        sums_of_rows = jnp.zeros((TILE, LANES), jnp.float32)
        for number in range(width // LANES):
            span = slice(number * LANES, (number + 1) * LANES)
            sums_of_rows = jnp.where(row == number + 1, sums[:, span], sums_of_rows)
    for slot in range(SIDE):
        factors = [(ref, start) for ref in (held[slot], other[-slot % SIDE]) for start in (0, tokens)]
        total = sum(
            jnp.dot(
                grads[table[SIDE + n]], ref[start : start + tokens, :], preferred_element_type=jnp.float32
            )
            for n, (ref, start) in enumerate(factors)
        )
        for part in range(total.shape[1] // LANES):
            bias = sums_of_rows if part == 0 else None
            pack(total[:, part * LANES : (part + 1) * LANES], bias, out, (table[slot], part))


def reduce(counts, *refs):
    messages, (out, bias_out) = refs[:-2], refs[-2:]
    rows = out.shape[1]
    at = 0
    for count in counts:
        mine, messages = messages[:count], messages[count:]
        sources = [(m, ()) for m in mine] if count > 1 else [(mine[0], (n,)) for n in range(SIDE)]
        if mine[0].shape[-2] == rows + EXTRA:
            bias_out[...] = sum(unpack_bias(m, (*n, 0), rows) for m, n in sources)
        for part in range(mine[0].shape[-3]):
            total = sum(unpack(m, (*n, part), rows) for m, n in sources)
            out[at : at + LANES, :] = total.T
            at += LANES


def whole():
    return pl.BlockSpec(memory_space=pltpu.VMEM)


def scalars():
    return pl.BlockSpec(memory_space=pltpu.SMEM)


def shape(dtype, *dims):
    return jax.ShapeDtypeStruct(dims, dtype)


def kernel(body, out_shape, scalar, *values, scratch=()):
    return pl.pallas_call(
        body,
        out_shape=out_shape,
        in_specs=[scalars()] * (scalar is not None) + [whole()] * len(values),
        out_specs=[whole()] * len(out_shape),
        scratch_shapes=scratch,
        compiler_params=PARAMS,
    )(*([] if scalar is None else [scalar]), *values)


def per_device(activations, out_grad, counts):
    rank, column = lax.axis_index("dp"), lax.axis_index("tensor")
    y, x, z, c = rank // SIDE, rank % SIDE, column // 2, column % 2
    tokens, width = out_grad.shape
    columns = activations.shape[1] // 4
    parts = columns // LANES
    slots = jnp.arange(SIDE)
    owners = jnp.where(c == 0, z - slots, z + slots) % SIDE
    ranks = (x - slots - 2 * c) % SIDE
    tables = [
        jnp.concatenate([numbers, ranks]).astype(jnp.int32) for numbers in (owners, (owners - y) % SIDE)
    ]
    halves = jnp.stack([x % 2, 1 - x % 2]).astype(jnp.int32)

    def to_owners(cuts, *others):
        got = [send(piece, perm) for piece, perm in zip(cuts, TO_OWNER, strict=True)]
        got[0] = after(got[0], *others)
        return kernel(join, [shape(got[0].dtype, 2 * tokens, columns)], None, *got)[0]

    def sums(table, grads, held, other, with_bias):
        (message,) = kernel(
            functools.partial(multiply, with_bias),
            [shape(jnp.int16, SIDE, parts, width + (EXTRA if with_bias else TILE), LANES)],
            table,
            grads,
            *held,
            *other,
        )
        return message

    cuts = kernel(cut, [shape(activations.dtype, tokens, columns)] * 4, halves, activations)
    (grad,) = kernel(
        mask,
        [shape(jnp.bfloat16, SIDE, width, tokens)],
        counts[rank].reshape(1),
        after(out_grad, *cuts),
    )
    own = [to_owners(cuts[:2], grad), to_owners(cuts[2:])]
    ring = [[piece, send(piece, RING_Z)] for piece in own]
    grads = swap_all(after(grad, *own), ALONG_X)
    other = [[send(piece, SWAP)] for piece in own]
    ring[0].append(send(ring[0][1], RING_Z))
    other[0].append(send(ring[0][1], SWAP))
    ring[1].append(send(after(ring[1][1], other[0][0]), RING_Z))
    other[1].append(send(ring[1][1], SWAP))
    ring[0].append(send(after(ring[0][2], other[0][1]), RING_Z))
    other[0].append(send(ring[0][2], SWAP))
    ring[1].append(send(after(ring[1][2], *other[1], other[0][2]), RING_Z))
    other[1].append(send(ring[1][2], SWAP))
    other[0].append(send(ring[0][3], SWAP))
    early = sums(tables[0], grads, ring[0], other[0], False)
    other[1].append(send(after(ring[1][3], early), SWAP))
    late = sums(tables[1], grads, ring[1], other[1], True)
    messages = [
        [swap_all(after(early, ring[1][3]), ALONG_Y)],
        [late[0]] + [send(late[d], AWAY_Y[d]) for d in range(1, SIDE)],
    ]
    weight_grad, bias = kernel(
        functools.partial(reduce, tuple(map(len, messages))),
        [shape(jnp.float32, 2 * columns, width), shape(jnp.float32, TILE, LANES)],
        None,
        *messages[0],
        *messages[1],
    )
    return weight_grad, bias[1 : 1 + width // LANES].reshape(width)


def solution(mesh):
    in_specs = (P("dp", "tensor"), P("dp", "tensor"), P())
    out_specs = (P("dp", "tensor"), P("tensor"))
    return jax.shard_map(
        per_device, mesh=mesh, in_specs=in_specs, out_specs=out_specs, check_vma=False
    )
```
